32 devices in a mesh: seq: 16 (over z, y, core), chan: 2 (over x).
Axes of the slice: x: 2, y: 2, z: 4, core: 2. Of those that a mesh axis runs over, the one named last changes fastest.
Arguments:
- tokens: bfloat16 [384, 512, 1024], P('chan', 'seq'), may hold values from -6 to 6
- gating: bfloat16 [384, 512, 1024], P(None, ('seq', 'chan')), may hold values from -6 to 6
- kernel: bfloat16 [384, 1024, 512], P('chan', 'seq'), may hold values from -6 to 6
- first_factor: bfloat16 [1024, 1024], replicated, may hold values from -0.1875 to 0.1875
- first_twiddle: float32 [512, 1024], P('seq'), may hold values from 0.5 to 1.5
- second_factor: bfloat16 [512, 512], replicated, may hold values from -0.25 to 0.25
- inverse_second: bfloat16 [512, 512], replicated, may hold values from -0.25 to 0.25
- inverse_twiddle: float32 [1024, 512], P('seq'), may hold values from 0.5 to 1.5
- inverse_first: bfloat16 [1024, 1024], replicated, may hold values from -0.1875 to 0.1875
- projection: bfloat16 [384, 384], replicated, may hold values from -0.3125 to 0.3125
Outputs:
- result: bfloat16 [384, 512, 1024], P(None, ('seq', 'chan'))
The draws below stay inside these ranges and needn't reach their ends.
All inputs are finite; a program needn't handle non-finite values.
Results may differ from the reference program's by a relative error of at most 0.012.
Values may be sent and summed in bfloat16 or wider, within the bound.
No kernel may reach another device: no remote copies, remote signals or barrier semaphores. Data moves between devices by JAX's collectives and lax.ppermute only.
A program may use at most 192 MiB of HBM per device.

```python
from functools import partial
import jax
import jax.numpy as jnp
from jax import lax

D = 384
A = 512
B = 1024


def block_levels(key, shape, split, smallest, top_value):
    factor_of, own = 1.0, jax.random.fold_in(key, 6)
    for axis_at, blocks in split:
        steps = jnp.exp(jax.random.uniform(jax.random.fold_in(own, axis_at), (blocks,), jnp.float32, smallest / len(split), top_value / len(split)))
        factor_of = factor_of * jnp.repeat(steps, shape[axis_at] // blocks).reshape([-1 if axis == axis_at else 1 for axis in range(len(shape))])
    return factor_of


def bell_draw(stream_key, shape, width, limit, pieces=(), kind=jnp.bfloat16):
    factor_of = block_levels(stream_key, shape, pieces, -0.22, 0.18) if pieces else 1.0
    values = jax.random.normal(stream_key, shape, jnp.float32) * width * factor_of
    return jnp.minimum(jnp.maximum(values, -limit), limit).astype(kind)


def setup_inputs(seed: int = 0) -> dict:
    streams_of = jax.random.split(jax.random.key(seed), 11)
    tokens = bell_draw(streams_of[0], (D, A, B), 1.0, 6.0, ((0, 2), (1, 16)))
    gating = bell_draw(streams_of[1], (D, A, B), 1.0, 6.0, ((1, 32),))
    kernel = bell_draw(streams_of[2], (D, B, A), 1.0, 6.0, ((0, 2), (1, 16)))
    first_factor = bell_draw(streams_of[3], (B, B), B ** -0.5, 0.1875)
    first_twiddle = jnp.clip(0.5 + 1.0 * jax.random.uniform(streams_of[4], (A, B), jnp.float32) ** block_levels(streams_of[4], (A, B), ((0, 16),), -0.2, 0.2), 0.5, 1.5)
    second_factor = bell_draw(streams_of[5], (A, A), A ** -0.5, 0.25)
    inverse_second = bell_draw(streams_of[6], (A, A), A ** -0.5, 0.25)
    inverse_twiddle = jnp.clip(0.5 + 1.0 * jax.random.uniform(streams_of[7], (B, A), jnp.float32) ** block_levels(streams_of[7], (B, A), ((0, 16),), -0.2, 0.2), 0.5, 1.5)
    inverse_first = bell_draw(streams_of[8], (B, B), B ** -0.5, 0.1875)
    projection = bell_draw(streams_of[9], (D, D), D ** -0.5, 0.3125)
    return dict(tokens=tokens, gating=gating, kernel=kernel, first_factor=first_factor, first_twiddle=first_twiddle, second_factor=second_factor, inverse_second=inverse_second, inverse_twiddle=inverse_twiddle, inverse_first=inverse_first, projection=projection)


def channel_mix(operands, first_factor, first_twiddle, second_factor, inverse_second, inverse_twiddle, inverse_first):
    signal, spectral, gate_plane = operands
    first = (jnp.dot(signal, first_factor.T, preferred_element_type=jnp.float32) * first_twiddle).astype(jnp.bfloat16)
    spectrum = jnp.dot(first.T, second_factor.T, preferred_element_type=jnp.float32)
    scaled = (spectrum * spectral.astype(jnp.float32)).astype(jnp.bfloat16)
    inverse = (jnp.dot(scaled, inverse_second.T, preferred_element_type=jnp.float32) * inverse_twiddle).astype(jnp.bfloat16)
    mixed = jnp.dot(inverse.T, inverse_first.T, preferred_element_type=jnp.float32).astype(jnp.bfloat16)
    return (mixed.astype(jnp.float32) * gate_plane.astype(jnp.float32)).astype(jnp.bfloat16)


def reference(tokens, gating, kernel, first_factor, first_twiddle, second_factor, inverse_second, inverse_twiddle, inverse_first, projection):
    mixer = partial(channel_mix, first_factor=first_factor, first_twiddle=first_twiddle, second_factor=second_factor, inverse_second=inverse_second, inverse_twiddle=inverse_twiddle, inverse_first=inverse_first)
    gated = lax.map(mixer, (tokens, kernel, gating))

    def project(rows):
        return jnp.dot(projection.T, rows, preferred_element_type=jnp.float32).astype(jnp.bfloat16)

    result = lax.map(project, jnp.swapaxes(gated, 0, 1))
    return jnp.swapaxes(result, 0, 1)
```

```python
from functools import partial

import jax
import jax.numpy as jnp
from jax import lax
from jax.experimental import pallas as pl
from jax.experimental.pallas import tpu as pltpu
from jax.sharding import PartitionSpec as P

LANES = 128
VMEM = 48 * 1024 * 1024
F32 = jnp.float32
BF16 = jnp.bfloat16


def largest_divisor(number, most):
    return max(d for d in range(1, min(number, most) + 1) if number % d == 0)


def dot_nt(left, right):
    return lax.dot_general(left, right, (((1,), (1,)), ((), ())), preferred_element_type=F32)


def regroup(tiles, width):
    count = len(tiles)
    if count == 1:
        return list(tiles)
    lane = lax.broadcasted_iota(jnp.int32, tiles[0].shape, tiles[0].ndim - 1)
    out = []
    for q in range(count):
        tile = None
        for r in range(count):
            shift = ((r - q) * width) % LANES
            moved = pltpu.roll(tiles[r], shift, tiles[r].ndim - 1) if shift else tiles[r]
            tile = moved if tile is None else jnp.where(lane >= r * width, moved, tile)
        out.append(tile)
    return out


def first_kernel(pack, width, tokens_ref, factor_ref, twiddle_ref, out_ref):
    channels, rows, order = tokens_ref.shape
    groups = channels // pack
    left = tokens_ref[...].reshape(channels * rows, order)
    step = 2 * LANES
    for at in range(0, order, step):
        part = dot_nt(left, factor_ref[at : at + step, :])
        part = part.reshape(channels, rows, step) * twiddle_ref[:, at : at + step][None]
        for half in range(step // LANES):
            tile = part[:, :, half * LANES : (half + 1) * LANES].reshape(groups, pack, rows, LANES)
            moved = regroup([tile[:, r].reshape(groups * rows, LANES) for r in range(pack)], width)
            base = (at // LANES + half) * pack
            for q in range(pack):
                out_ref[base + q] = moved[q].astype(BF16).reshape(groups, rows, LANES)


def middle_kernel(pack, recv_ref, kernel_ref, second_ref, back_ref, twiddle_ref, out_ref):
    sources, groups, rows, _ = recv_ref.shape
    dests, _, out_rows, _ = out_ref.shape
    outer = second_ref.shape[0]
    width = kernel_ref.shape[1]
    both = 2 if groups % 2 == 0 else 1
    for at in range(0, groups, both):
        cols = [recv_ref[:, at + p].reshape(sources * rows, LANES) for p in range(both)]
        spectrum = jnp.dot(
            second_ref[...], jnp.concatenate(cols, axis=1), preferred_element_type=F32
        )
        kern = [
            kernel_ref[(at + p) * pack : (at + p + 1) * pack].reshape(pack * width, outer).astype(F32).T
            for p in range(both)
        ]
        scaled = (spectrum * jnp.concatenate(kern, axis=1)).astype(BF16)
        inverse = jnp.dot(back_ref[...], scaled, preferred_element_type=F32)
        for p in range(both):
            part = inverse[:, p * LANES : (p + 1) * LANES] * twiddle_ref[...]
            out_ref[:, at + p] = part.astype(BF16).reshape(dests, out_rows, LANES)


def last_kernel(pack, width, recv_ref, factor_ref, gating_ref, out_ref, wide_ref):
    sources, _, groups, rows, _ = recv_ref.shape
    order = factor_ref.shape[0]
    for t in range(sources // pack):
        tiles = [
            recv_ref[t * pack + r, 0].astype(F32).reshape(groups * rows, LANES) for r in range(pack)
        ]
        moved = regroup(tiles, width)
        for q in range(pack):
            wide_ref[:, q, :, t * LANES : (t + 1) * LANES] = moved[q].astype(BF16).reshape(groups, rows, LANES)
    left = wide_ref[...].reshape(groups * pack * rows, order)
    step = 2 * LANES
    for at in range(0, order, step):
        mixed = dot_nt(left, factor_ref[at : at + step, :]).astype(BF16)
        mixed = mixed.reshape(groups * pack, rows, step).astype(F32)
        gated = mixed * gating_ref[0, :, :, at : at + step].astype(F32)
        out_ref[0, :, :, at : at + step] = gated.astype(BF16)


def project_kernel(count, *refs):
    gated_refs, (projection_ref, out_ref, left_ref, right_ref) = refs[:count], refs[count:]
    parts, channels, rows, step = gated_refs[0].shape
    total = projection_ref.shape[0]
    tiles = step // LANES
    for g, ref in enumerate(gated_refs):
        for x in range(parts):
            start = (x * (total // parts) + g * channels) * rows
            for t in range(tiles):
                left_ref[t, start : start + channels * rows, :] = (
                    ref[x, :, :, t * LANES : (t + 1) * LANES].astype(F32).reshape(channels * rows, LANES)
                )
    for i in range(rows):
        right = jnp.concatenate(
            [left_ref[t, pl.ds(i, total, stride=rows), :].astype(BF16) for t in range(tiles)], axis=1
        )
        done = jnp.dot(projection_ref[...], right, preferred_element_type=F32)
        for t in range(tiles):
            right_ref[t, pl.ds(i, total, stride=rows), :] = done[:, t * LANES : (t + 1) * LANES]
    for t in range(tiles):
        out_ref[:, :, t * LANES : (t + 1) * LANES] = right_ref[t].reshape(total, rows, LANES).astype(BF16)


def params(grid):
    return pltpu.CompilerParams(
        vmem_limit_bytes=VMEM, dimension_semantics=("arbitrary",) * len(grid)
    )


def first_step(tokens, factor, twiddle, at, count, sources):
    channels, rows, order = tokens.shape
    width = order // sources
    pack = LANES // width
    per = pack * largest_divisor(count // pack, 16 // pack)
    grid = (count // per,)
    return pl.pallas_call(
        partial(first_kernel, pack, width),
        grid=grid,
        in_specs=[
            pl.BlockSpec((per, rows, order), lambda n: (at // per + n, 0, 0)),
            pl.BlockSpec(factor.shape, lambda n: (0, 0)),
            pl.BlockSpec(twiddle.shape, lambda n: (0, 0)),
        ],
        out_specs=pl.BlockSpec((sources, per // pack, rows, LANES), lambda n: (0, n, 0, 0)),
        out_shape=jax.ShapeDtypeStruct((sources, count // pack, rows, LANES), BF16),
        compiler_params=params(grid),
        cost_estimate=pl.CostEstimate(
            flops=2 * count * rows * order * order, bytes_accessed=4 * count * rows * order, transcendentals=0
        ),
        name="first_factor",
    )(tokens, factor, twiddle)


def middle_step(received, kernel, second, back, twiddle, at, dests):
    sources, groups, rows, _ = received.shape
    channels, width, outer = kernel.shape
    pack = LANES // width
    per = largest_divisor(groups, 6)
    grid = (groups // per,)
    out_rows = outer // dests
    return pl.pallas_call(
        partial(middle_kernel, pack),
        grid=grid,
        in_specs=[
            pl.BlockSpec((sources, per, rows, LANES), lambda n: (0, n, 0, 0)),
            pl.BlockSpec((per * pack, width, outer), lambda n: (at // (per * pack) + n, 0, 0)),
            pl.BlockSpec(second.shape, lambda n: (0, 0)),
            pl.BlockSpec(back.shape, lambda n: (0, 0)),
            pl.BlockSpec(twiddle.shape, lambda n: (0, 0)),
        ],
        out_specs=pl.BlockSpec((dests, per, out_rows, LANES), lambda n: (0, n, 0, 0)),
        out_shape=jax.ShapeDtypeStruct((dests, groups, out_rows, LANES), BF16),
        compiler_params=params(grid),
        cost_estimate=pl.CostEstimate(
            flops=4 * groups * LANES * outer * outer, bytes_accessed=6 * groups * LANES * outer, transcendentals=0
        ),
        name="outer_factors",
    )(received, kernel, second, back, twiddle)


def last_step(returned, factor, gating, at, sources):
    _, parts, groups, rows, _ = returned.shape
    order = factor.shape[0]
    width = order // sources
    pack = LANES // width
    per = largest_divisor(groups, 32 // pack)
    grid = (parts, groups // per)
    return pl.pallas_call(
        partial(last_kernel, pack, width),
        grid=grid,
        in_specs=[
            pl.BlockSpec((sources, 1, per, rows, LANES), lambda x, n: (0, x, n, 0, 0)),
            pl.BlockSpec(factor.shape, lambda x, n: (0, 0)),
            pl.BlockSpec((1, per * pack, rows, order), lambda x, n: (x, at // (per * pack) + n, 0, 0)),
        ],
        out_specs=pl.BlockSpec((1, per * pack, rows, order), lambda x, n: (x, n, 0, 0)),
        out_shape=jax.ShapeDtypeStruct((parts, groups * pack, rows, order), BF16),
        scratch_shapes=[pltpu.VMEM((per, pack, rows, order), BF16)],
        compiler_params=params(grid),
        cost_estimate=pl.CostEstimate(
            flops=2 * parts * groups * pack * rows * order * order,
            bytes_accessed=6 * parts * groups * pack * rows * order,
            transcendentals=0,
        ),
        name="last_factor",
    )(returned, factor, gating)


def project_step(gated, projection):
    parts, channels, rows, order = gated[0].shape
    total = projection.shape[0]
    step = 2 * LANES
    grid = (order // step,)
    return pl.pallas_call(
        partial(project_kernel, len(gated)),
        grid=grid,
        in_specs=[pl.BlockSpec((parts, channels, rows, step), lambda n: (0, 0, 0, n)) for _ in gated]
        + [pl.BlockSpec(projection.shape, lambda n: (0, 0))],
        out_specs=pl.BlockSpec((total, rows, step), lambda n: (0, 0, n)),
        out_shape=jax.ShapeDtypeStruct((total, rows, order), BF16),
        scratch_shapes=[pltpu.VMEM((step // LANES, total * rows, LANES), F32)] * 2,
        compiler_params=params(grid),
        cost_estimate=pl.CostEstimate(
            flops=2 * total * total * rows * order, bytes_accessed=4 * total * rows * order, transcendentals=0
        ),
        name="projection",
    )(*gated, projection)


def chunked(
    tokens,
    gating,
    kernel,
    first_factor,
    first_twiddle,
    second_factor,
    inverse_second,
    inverse_twiddle,
    inverse_first,
    projection,
):
    sources, parts = lax.axis_size("seq"), lax.axis_size("chan")
    dests = sources * parts
    channels, _, order = tokens.shape
    width = order // sources
    pack = LANES // width
    total, out_rows, _ = gating.shape
    gating = gating.reshape(parts, channels, out_rows, order)
    twiddle_back = jnp.tile(inverse_twiddle.T, (1, pack))
    projection = projection.T
    chunks = 4
    count = channels // chunks
    received = []
    for g in range(chunks):
        sent = first_step(tokens, first_factor, first_twiddle, g * count, count, sources)
        received.append(lax.all_to_all(sent, "seq", split_axis=0, concat_axis=0, tiled=True))
    returned = []
    for g in range(chunks):
        sent = middle_step(
            received[g], kernel, second_factor, inverse_second, twiddle_back, g * count, dests
        )
        returned.append(lax.all_to_all(sent, ("seq", "chan"), split_axis=0, concat_axis=0, tiled=True))
    gated = []
    for g in range(chunks):
        back = returned[g].reshape(sources, parts, count // pack, out_rows, LANES)
        gated.append(last_step(back, inverse_first, gating, g * count, sources))
    return project_step(gated, projection)


def plain(
    tokens,
    gating,
    kernel,
    first_factor,
    first_twiddle,
    second_factor,
    inverse_second,
    inverse_twiddle,
    inverse_first,
    projection,
):
    seq_count = lax.axis_size("seq")
    chan_count = lax.axis_size("chan")
    channels, local_rows, order_inner = tokens.shape
    order_outer = second_factor.shape[0]
    block_cols = order_inner // seq_count
    chan_rows = local_rows // chan_count
    first_split = first_factor.reshape(seq_count, block_cols, order_inner)
    forward = jnp.einsum("cab,skb->scka", tokens, first_split, preferred_element_type=jnp.float32)
    twiddle = first_twiddle.reshape(local_rows, seq_count, block_cols).transpose(1, 2, 0)
    forward = (forward * twiddle[:, None]).astype(jnp.bfloat16)
    forward = forward.reshape(seq_count, 1, channels, block_cols * local_rows)
    received = lax.all_to_all(forward, "seq", split_axis=0, concat_axis=1, tiled=True)
    received = received.reshape(seq_count, channels, block_cols, local_rows)
    second_split = second_factor.reshape(order_outer, seq_count, local_rows)
    spectrum = jnp.einsum(
        "scka,jsa->ckj", received, second_split, preferred_element_type=jnp.float32
    )
    scaled = (spectrum * kernel).astype(jnp.bfloat16)
    first_join = inverse_first.reshape(order_inner, seq_count, block_cols)
    inverse_split = inverse_second.reshape(seq_count, local_rows, order_outer)
    inverse = jnp.einsum("ckj,sij->scki", scaled, inverse_split, preferred_element_type=jnp.float32)
    twiddle_back = inverse_twiddle.reshape(block_cols, seq_count, local_rows).transpose(1, 0, 2)
    inverse = (inverse * twiddle_back[:, None]).astype(jnp.bfloat16)
    inverse = inverse.reshape(seq_count, 1, channels, block_cols * local_rows)
    returned = lax.all_to_all(inverse, "seq", split_axis=0, concat_axis=1, tiled=True)
    returned = returned.reshape(seq_count, channels, block_cols, local_rows)
    mixed_rows = jnp.einsum(
        "scki,bsk->cib", returned, first_join, preferred_element_type=jnp.float32
    ).astype(jnp.bfloat16)
    mixed_rows = mixed_rows.reshape(channels, chan_count, chan_rows, order_inner)
    mixed_rows = lax.all_to_all(mixed_rows, "chan", split_axis=1, concat_axis=0, tiled=True)
    mixed_rows = mixed_rows.reshape(channels * chan_count, chan_rows, order_inner)
    gated_rows = (mixed_rows.astype(jnp.float32) * gating.astype(jnp.float32)).astype(jnp.bfloat16)
    result_rows = jnp.einsum(
        "cab,ce->eab", gated_rows, projection, preferred_element_type=jnp.float32
    )
    return result_rows.astype(jnp.bfloat16)


def body(*arrays):
    tokens, gating = arrays[:2]
    width = tokens.shape[2] // lax.axis_size("seq")
    whole_tiles = gating.shape[1] % 16 == 0 and tokens.shape[1] % 16 == 0 and LANES % width == 0
    return chunked(*arrays) if whole_tiles else plain(*arrays)


def solution(mesh):
    return jax.shard_map(
        body,
        mesh=mesh,
        in_specs=(
            P("chan", "seq", None),
            P(None, ("seq", "chan"), None),
            P("chan", "seq", None),
            P(),
            P("seq", None),
            P(),
            P(),
            P("seq", None),
            P(),
            P(),
        ),
        out_specs=P(None, ("seq", "chan"), None),
        check_vma=False,
    )
```

```python
from functools import partial

import jax
import jax.numpy as jnp
from jax import lax
from jax.experimental import pallas as pl
from jax.experimental.pallas import tpu as pltpu
from jax.sharding import PartitionSpec as P

LANES = 128
SUBLANES = 8
GROUPS = 16
FIRST = 16
MIB = 1024 * 1024
F32 = jnp.float32
BF16 = jnp.bfloat16


def largest_divisor(number, most):
    return max(d for d in range(1, min(number, most) + 1) if number % d == 0)


def dot_nt(left, right):
    return lax.dot_general(left, right, (((1,), (1,)), ((), ())), preferred_element_type=F32)


def regroup(tiles, width):
    count = len(tiles)
    if count == 1:
        return list(tiles)
    lane = lax.broadcasted_iota(jnp.int32, tiles[0].shape, tiles[0].ndim - 1)
    out = []
    for q in range(count):
        tile = None
        for r in range(count):
            shift = ((r - q) * width) % LANES
            moved = pltpu.roll(tiles[r], shift, tiles[r].ndim - 1) if shift else tiles[r]
            tile = moved if tile is None else jnp.where(lane >= r * width, moved, tile)
        out.append(tile)
    return out


def first_kernel(pack, width, tokens_ref, factor_ref, twiddle_ref, out_ref):
    channels, rows, order = tokens_ref.shape
    groups = channels // pack
    left = tokens_ref[...].reshape(channels * rows, order)
    step = 2 * LANES
    for at in range(0, order, step):
        part = dot_nt(left, factor_ref[at : at + step, :])
        part = part.reshape(channels, rows, step) * twiddle_ref[:, at : at + step][None]
        for half in range(step // LANES):
            tile = part[:, :, half * LANES : (half + 1) * LANES].reshape(groups, pack, rows, LANES)
            moved = regroup([tile[:, r].reshape(groups * rows, LANES) for r in range(pack)], width)
            base = (at // LANES + half) * pack
            for q in range(pack):
                out_ref[base + q] = moved[q].astype(BF16).reshape(groups, rows, LANES)


def middle_kernel(pack, recv_ref, kernel_ref, second_ref, back_ref, twiddle_ref, out_ref, turn_ref):
    size = second_ref.shape[0]
    groups = recv_ref.shape[1]
    width = kernel_ref.shape[1]
    both = 2 if groups % 2 == 0 else 1
    for at in range(0, groups, both):
        cols = [recv_ref[:, at + p].reshape(size, LANES) for p in range(both)]
        spectrum = jnp.dot(
            second_ref[...], jnp.concatenate(cols, axis=1), preferred_element_type=F32
        )
        kern = [
            kernel_ref[(at + p) * pack : (at + p + 1) * pack].reshape(pack * width, size).astype(F32).T
            for p in range(both)
        ]
        scaled = (spectrum * jnp.concatenate(kern, axis=1)).astype(BF16)
        inverse = jnp.dot(back_ref[...], scaled, preferred_element_type=F32)
        for p in range(both):
            part = inverse[:, p * LANES : (p + 1) * LANES] * twiddle_ref[...]
            turn_ref[pl.ds(at + p, size, stride=groups), :] = part
    out_ref[...] = turn_ref[...].astype(BF16).reshape(out_ref.shape)


def turn_kernel(pack, gating_ref, out_ref, turn_ref):
    channels, rows, order = gating_ref.shape
    groups = channels // pack
    for t in range(order // LANES):
        lanes = slice(t * LANES, (t + 1) * LANES)
        turn_ref[t] = gating_ref[:, :, lanes].astype(F32).reshape(channels * rows, LANES)
        for r in range(pack):
            for i in range(rows):
                part = turn_ref[t, pl.ds(r * rows + i, groups, stride=pack * rows), :]
                out_ref[0, r, i, :, lanes] = part.astype(BF16)


def last_kernel(pack, width, recv_ref, factor_ref, gating_ref, out_ref, wide_ref):
    sources, _, rows, groups, _ = recv_ref.shape
    order = factor_ref.shape[0]
    widen(pack, width, recv_ref.at[:, 0], wide_ref)
    left = wide_ref[...].reshape(pack * rows * groups, order)
    step = 2 * LANES
    for at in range(0, order, step):
        mixed = jnp.dot(left, factor_ref[:, at : at + step], preferred_element_type=F32)
        mixed = mixed.astype(BF16).astype(F32)
        mixed = mixed.reshape(pack, rows, groups, step)
        gated = mixed * gating_ref[0, 0, :, :, :, at : at + step].astype(F32)
        out_ref[0, 0, :, :, :, at : at + step] = gated.astype(BF16)


def widen(pack, width, recv, wide_ref):
    sources, rows, groups, _ = recv.shape
    for t in range(sources // pack):
        tiles = [recv[t * pack + r].astype(F32).reshape(rows * groups, LANES) for r in range(pack)]
        moved = regroup(tiles, width)
        for q in range(pack):
            wide_ref[q, :, t * LANES : (t + 1) * LANES] = moved[q].astype(BF16)


def project_kernel(count, *refs):
    gated_refs, (projection_ref, out_ref, turn_ref) = refs[:count], refs[count:]
    parts, _, pack, rows, _, step = gated_refs[0].shape
    total = projection_ref.shape[0]
    tiles = step // LANES
    for i in range(rows):
        right = jnp.concatenate(
            [
                ref[x, n, r, i]
                for x in range(parts)
                for ref in gated_refs
                for n in range(ref.shape[1])
                for r in range(pack)
            ],
            axis=0,
        )
        done = jnp.dot(projection_ref[...], right, preferred_element_type=F32)
        for t in range(tiles):
            turn_ref[t, i // SUBLANES, pl.ds(i % SUBLANES, total, stride=SUBLANES), :] = done[
                :, t * LANES : (t + 1) * LANES
            ]
    some = largest_divisor(total, 32)
    for t in range(tiles):
        for e in range(0, total, some):
            halves = [
                turn_ref[t, h, e * SUBLANES : (e + some) * SUBLANES].reshape(some, SUBLANES, LANES)
                for h in range(rows // SUBLANES)
            ]
            out_ref[e : e + some, :, t * LANES : (t + 1) * LANES] = jnp.concatenate(halves, axis=1).astype(BF16)


def params(grid, mib):
    return pltpu.CompilerParams(
        vmem_limit_bytes=mib * MIB, dimension_semantics=("arbitrary",) * len(grid)
    )


def first_step(tokens, factor, twiddle, at, count, sources):
    channels, rows, order = tokens.shape
    width = order // sources
    pack = LANES // width
    per = pack * largest_divisor(count // pack, FIRST // pack)
    grid = (count // per,)
    return pl.pallas_call(
        partial(first_kernel, pack, width),
        grid=grid,
        in_specs=[
            pl.BlockSpec((per, rows, order), lambda n: (at // per + n, 0, 0)),
            pl.BlockSpec(factor.shape, lambda n: (0, 0)),
            pl.BlockSpec(twiddle.shape, lambda n: (0, 0)),
        ],
        out_specs=pl.BlockSpec((sources, per // pack, rows, LANES), lambda n: (0, n, 0, 0)),
        out_shape=jax.ShapeDtypeStruct((sources, count // pack, rows, LANES), BF16),
        compiler_params=params(grid, 60),
        cost_estimate=pl.CostEstimate(
            flops=2 * count * rows * order * order, bytes_accessed=4 * count * rows * order, transcendentals=0
        ),
        name="first_factor",
    )(tokens, factor, twiddle)


def middle_step(received, kernel, second, back, twiddle, offset, at, count, dests):
    sources, _, rows, _ = received.shape
    channels, width, size = kernel.shape
    pack = LANES // width
    per = GROUPS
    groups = count // pack
    grid = (groups // per,)
    out_rows = size // dests
    return pl.pallas_call(
        partial(middle_kernel, pack),
        grid=grid,
        in_specs=[
            pl.BlockSpec((sources, per, rows, LANES), lambda n: (0, offset // (per * pack) + n, 0, 0)),
            pl.BlockSpec((per * pack, width, size), lambda n: (at // (per * pack) + n, 0, 0)),
            pl.BlockSpec(second.shape, lambda n: (0, 0)),
            pl.BlockSpec(back.shape, lambda n: (0, 0)),
            pl.BlockSpec(twiddle.shape, lambda n: (0, 0)),
        ],
        out_specs=pl.BlockSpec((dests, out_rows, per, LANES), lambda n: (0, 0, n, 0)),
        out_shape=jax.ShapeDtypeStruct((dests, out_rows, groups, LANES), BF16),
        scratch_shapes=[pltpu.VMEM((size * per, LANES), F32)],
        compiler_params=params(grid, 32),
        cost_estimate=pl.CostEstimate(
            flops=4 * groups * LANES * size * size, bytes_accessed=6 * groups * LANES * size, transcendentals=0
        ),
        name="outer_factors",
    )(received, kernel, second, back, twiddle)


def turn_step(gating, pack):
    total, rows, order = gating.shape
    per = GROUPS * pack
    grid = (total // per,)
    return pl.pallas_call(
        partial(turn_kernel, pack),
        grid=grid,
        in_specs=[pl.BlockSpec((per, rows, order), lambda n: (n, 0, 0))],
        out_specs=pl.BlockSpec((1, pack, rows, GROUPS, order), lambda n: (n, 0, 0, 0, 0)),
        out_shape=jax.ShapeDtypeStruct((total // per, pack, rows, GROUPS, order), BF16),
        scratch_shapes=[pltpu.VMEM((order // LANES, per * rows, LANES), F32)],
        compiler_params=params(grid, 32),
        cost_estimate=pl.CostEstimate(
            flops=total * rows * order, bytes_accessed=4 * total * rows * order, transcendentals=0
        ),
        name="turn_gating",
    )(gating)


def last_step(returned, factor, gating, at, sources):
    _, parts, rows, groups, _ = returned.shape
    order = factor.shape[0]
    width = order // sources
    pack = LANES // width
    per = GROUPS
    grid = (parts, groups // per)
    block = (1, 1, pack, rows, per, order)
    return pl.pallas_call(
        partial(last_kernel, pack, width),
        grid=grid,
        in_specs=[
            pl.BlockSpec((sources, 1, rows, per, LANES), lambda x, n: (0, x, 0, n, 0)),
            pl.BlockSpec(factor.shape, lambda x, n: (0, 0)),
            pl.BlockSpec(block, lambda x, n: (x, at // (per * pack) + n, 0, 0, 0, 0)),
        ],
        out_specs=pl.BlockSpec(block, lambda x, n: (x, n, 0, 0, 0, 0)),
        out_shape=jax.ShapeDtypeStruct((parts, groups // per, pack, rows, per, order), BF16),
        scratch_shapes=[pltpu.VMEM((pack, rows * per, order), BF16)],
        compiler_params=params(grid, 32),
        cost_estimate=pl.CostEstimate(
            flops=2 * parts * groups * pack * rows * order * order,
            bytes_accessed=6 * parts * groups * pack * rows * order,
            transcendentals=0,
        ),
        name="last_factor",
    )(returned, factor, gating)


def project_step(gated, projection):
    _, _, _, rows, _, order = gated[0].shape
    total = projection.shape[0]
    step = 2 * LANES
    grid = (order // step,)
    return pl.pallas_call(
        partial(project_kernel, len(gated)),
        grid=grid,
        in_specs=[
            pl.BlockSpec(part.shape[:-1] + (step,), lambda n: (0, 0, 0, 0, 0, n)) for part in gated
        ]
        + [pl.BlockSpec(projection.shape, lambda n: (0, 0))],
        out_specs=pl.BlockSpec((total, rows, step), lambda n: (0, 0, n)),
        out_shape=jax.ShapeDtypeStruct((total, rows, order), BF16),
        scratch_shapes=[
            pltpu.VMEM((step // LANES, rows // SUBLANES, total * SUBLANES, LANES), F32),
        ],
        compiler_params=params(grid, 28),
        cost_estimate=pl.CostEstimate(
            flops=2 * total * total * rows * order, bytes_accessed=4 * total * rows * order, transcendentals=0
        ),
        name="projection",
    )(*gated, projection)


def spans(sizes):
    at = 0
    for size in sizes:
        yield at, size
        at += size


def chunked(
    tokens,
    gating,
    kernel,
    first_factor,
    first_twiddle,
    second_factor,
    inverse_second,
    inverse_twiddle,
    inverse_first,
    projection,
):
    sources, parts = lax.axis_size("seq"), lax.axis_size("chan")
    dests = sources * parts
    channels, _, order = tokens.shape
    width = order // sources
    pack = LANES // width
    unit = GROUPS * pack
    units = channels // unit
    total, out_rows, _ = gating.shape
    inverse_first = inverse_first.T
    twiddle_back = jnp.tile(inverse_twiddle.T, (1, pack))
    projection = projection.T.reshape(total, total // unit, GROUPS, pack)
    projection = projection.transpose(0, 1, 3, 2).reshape(total, total)
    there = [unit, channels - unit] if units > 1 else [unit]
    back = [unit, channels - 2 * unit, unit] if units > 2 else [unit] * units

    turned = turn_step(gating, pack).reshape(parts, units, pack, out_rows, GROUPS, order)
    starts, arrived = [], []

    def exchange(sent, axes):
        if arrived:
            sent, arrived[-1] = lax.optimization_barrier((sent, arrived[-1]))
        arrived.append(lax.all_to_all(sent, axes, split_axis=0, concat_axis=0, tiled=True))

    for at, count in spans(there):
        starts.append(at)
        exchange(first_step(tokens, first_factor, first_twiddle, at, count, sources), "seq")
    for at, count in spans(back):
        n = max(n for n, start in enumerate(starts) if start <= at)
        sent = middle_step(
            arrived[n], kernel, second_factor, inverse_second, twiddle_back, at - starts[n], at, count, dests
        )
        if at > 0 and at + count == channels:
            sent, turned = lax.optimization_barrier((sent, turned))
        exchange(sent, ("seq", "chan"))
    returned = arrived[len(there) :]
    gated = []
    for (at, count), block in zip(spans(back), returned, strict=True):
        block = block.reshape(sources, parts, out_rows, count // pack, LANES)
        gated.append(last_step(block, inverse_first, turned, at, sources))
    return project_step(gated, projection)


def plain(
    tokens,
    gating,
    kernel,
    first_factor,
    first_twiddle,
    second_factor,
    inverse_second,
    inverse_twiddle,
    inverse_first,
    projection,
):
    seq_count = lax.axis_size("seq")
    chan_count = lax.axis_size("chan")
    channels, local_rows, order_inner = tokens.shape
    order_outer = second_factor.shape[0]
    block_cols = order_inner // seq_count
    chan_rows = local_rows // chan_count
    first_split = first_factor.reshape(seq_count, block_cols, order_inner)
    forward = jnp.einsum("cab,skb->scka", tokens, first_split, preferred_element_type=jnp.float32)
    twiddle = first_twiddle.reshape(local_rows, seq_count, block_cols).transpose(1, 2, 0)
    forward = (forward * twiddle[:, None]).astype(jnp.bfloat16)
    forward = forward.reshape(seq_count, 1, channels, block_cols * local_rows)
    received = lax.all_to_all(forward, "seq", split_axis=0, concat_axis=1, tiled=True)
    received = received.reshape(seq_count, channels, block_cols, local_rows)
    second_split = second_factor.reshape(order_outer, seq_count, local_rows)
    spectrum = jnp.einsum(
        "scka,jsa->ckj", received, second_split, preferred_element_type=jnp.float32
    )
    scaled = (spectrum * kernel).astype(jnp.bfloat16)
    first_join = inverse_first.reshape(order_inner, seq_count, block_cols)
    inverse_split = inverse_second.reshape(seq_count, local_rows, order_outer)
    inverse = jnp.einsum("ckj,sij->scki", scaled, inverse_split, preferred_element_type=jnp.float32)
    twiddle_back = inverse_twiddle.reshape(block_cols, seq_count, local_rows).transpose(1, 0, 2)
    inverse = (inverse * twiddle_back[:, None]).astype(jnp.bfloat16)
    inverse = inverse.reshape(seq_count, 1, channels, block_cols * local_rows)
    returned = lax.all_to_all(inverse, "seq", split_axis=0, concat_axis=1, tiled=True)
    returned = returned.reshape(seq_count, channels, block_cols, local_rows)
    mixed_rows = jnp.einsum(
        "scki,bsk->cib", returned, first_join, preferred_element_type=jnp.float32
    ).astype(jnp.bfloat16)
    mixed_rows = mixed_rows.reshape(channels, chan_count, chan_rows, order_inner)
    mixed_rows = lax.all_to_all(mixed_rows, "chan", split_axis=1, concat_axis=0, tiled=True)
    mixed_rows = mixed_rows.reshape(channels * chan_count, chan_rows, order_inner)
    gated_rows = (mixed_rows.astype(jnp.float32) * gating.astype(jnp.float32)).astype(jnp.bfloat16)
    result_rows = jnp.einsum(
        "cab,ce->eab", gated_rows, projection, preferred_element_type=jnp.float32
    )
    return result_rows.astype(jnp.bfloat16)


def body(*arrays):
    tokens, gating = arrays[:2]
    width = tokens.shape[2] // lax.axis_size("seq")
    whole_tiles = gating.shape[1] % 16 == 0 and tokens.shape[1] % 16 == 0 and LANES % width == 0
    whole_tiles = whole_tiles and tokens.shape[0] % (GROUPS * LANES // width) == 0
    return chunked(*arrays) if whole_tiles else plain(*arrays)


def solution(mesh):
    return jax.shard_map(
        body,
        mesh=mesh,
        in_specs=(
            P("chan", "seq", None),
            P(None, ("seq", "chan"), None),
            P("chan", "seq", None),
            P(),
            P("seq", None),
            P(),
            P(),
            P("seq", None),
            P(),
            P(),
        ),
        out_specs=P(None, ("seq", "chan"), None),
        check_vma=False,
    )
```

```python
from functools import partial

import jax
import jax.numpy as jnp
from jax import lax
from jax.experimental import pallas as pl
from jax.experimental.pallas import tpu as pltpu
from jax.sharding import PartitionSpec as P

LANES = 128
SUBLANES = 8
GROUPS = 16
FIRST = 16
MIB = 1024 * 1024
F32 = jnp.float32
BF16 = jnp.bfloat16


def largest_divisor(number, most):
    return max(d for d in range(1, min(number, most) + 1) if number % d == 0)


def dot_nt(left, right):
    return lax.dot_general(left, right, (((1,), (1,)), ((), ())), preferred_element_type=F32)


def regroup(tiles, width):
    count = len(tiles)
    if count == 1:
        return list(tiles)
    lane = lax.broadcasted_iota(jnp.int32, tiles[0].shape, tiles[0].ndim - 1)
    out = []
    for q in range(count):
        tile = None
        for r in range(count):
            shift = ((r - q) * width) % LANES
            moved = pltpu.roll(tiles[r], shift, tiles[r].ndim - 1) if shift else tiles[r]
            tile = moved if tile is None else jnp.where(lane >= r * width, moved, tile)
        out.append(tile)
    return out


def first_kernel(pack, width, tokens_ref, factor_ref, twiddle_ref, out_ref):
    channels, rows, order = tokens_ref.shape
    groups = channels // pack
    left = tokens_ref[...].reshape(channels * rows, order)
    step = 2 * LANES
    for at in range(0, order, step):
        part = dot_nt(left, factor_ref[at : at + step, :])
        part = part.reshape(channels, rows, step) * twiddle_ref[:, at : at + step][None]
        for half in range(step // LANES):
            tile = part[:, :, half * LANES : (half + 1) * LANES].reshape(groups, pack, rows, LANES)
            moved = regroup([tile[:, r].reshape(groups * rows, LANES) for r in range(pack)], width)
            base = (at // LANES + half) * pack
            for q in range(pack):
                out_ref[base + q] = moved[q].astype(BF16).reshape(groups, rows, LANES)


def middle_kernel(pack, recv_ref, kernel_ref, second_ref, back_ref, twiddle_ref, out_ref, turn_ref):
    size = second_ref.shape[0]
    groups = recv_ref.shape[1]
    width = kernel_ref.shape[1]
    both = 2 if groups % 2 == 0 else 1
    for at in range(0, groups, both):
        cols = [recv_ref[:, at + p].reshape(size, LANES) for p in range(both)]
        spectrum = jnp.dot(
            second_ref[...], jnp.concatenate(cols, axis=1), preferred_element_type=F32
        )
        kern = [
            kernel_ref[(at + p) * pack : (at + p + 1) * pack].reshape(pack * width, size).astype(F32).T
            for p in range(both)
        ]
        scaled = (spectrum * jnp.concatenate(kern, axis=1)).astype(BF16)
        inverse = jnp.dot(back_ref[...], scaled, preferred_element_type=F32)
        for p in range(both):
            part = inverse[:, p * LANES : (p + 1) * LANES] * twiddle_ref[...]
            turn_ref[pl.ds(at + p, size, stride=groups), :] = part
    out_ref[...] = turn_ref[...].astype(BF16).reshape(out_ref.shape)


def turn_kernel(pack, gating_ref, out_ref, turn_ref):
    _, channels, rows, order = gating_ref.shape
    groups = channels // pack
    for t in range(order // LANES):
        lanes = slice(t * LANES, (t + 1) * LANES)
        turn_ref[t] = gating_ref[0, :, :, lanes].astype(F32).reshape(channels * rows, LANES)
        for r in range(pack):
            for i in range(rows):
                part = turn_ref[t, pl.ds(r * rows + i, groups, stride=pack * rows), :]
                out_ref[0, 0, r, i, :, lanes] = part.astype(BF16)


def last_kernel(pack, width, recv_ref, factor_ref, gating_ref, out_ref, wide_ref):
    sources, _, rows, groups, _ = recv_ref.shape
    order = factor_ref.shape[0]
    widen(pack, width, recv_ref.at[:, 0], wide_ref)
    left = wide_ref[...].reshape(pack * rows * groups, order)
    step = 2 * LANES
    for at in range(0, order, step):
        mixed = jnp.dot(left, factor_ref[:, at : at + step], preferred_element_type=F32)
        mixed = mixed.astype(BF16).astype(F32)
        mixed = mixed.reshape(pack, rows, groups, step)
        gated = mixed * gating_ref[0, 0, :, :, :, at : at + step].astype(F32)
        out_ref[0, 0, :, :, :, at : at + step] = gated.astype(BF16)


def widen(pack, width, recv, wide_ref):
    sources, rows, groups, _ = recv.shape
    for t in range(sources // pack):
        tiles = [recv[t * pack + r].astype(F32).reshape(rows * groups, LANES) for r in range(pack)]
        moved = regroup(tiles, width)
        for q in range(pack):
            wide_ref[q, :, t * LANES : (t + 1) * LANES] = moved[q].astype(BF16)


def project_kernel(count, *refs):
    gated_refs, (projection_ref, out_ref, turn_ref) = refs[:count], refs[count:]
    parts, _, pack, rows, _, step = gated_refs[0].shape
    total = projection_ref.shape[0]
    tiles = step // LANES
    for i in range(rows):
        right = jnp.concatenate(
            [
                ref[x, n, r, i]
                for x in range(parts)
                for ref in gated_refs
                for n in range(ref.shape[1])
                for r in range(pack)
            ],
            axis=0,
        )
        done = jnp.dot(projection_ref[...], right, preferred_element_type=F32)
        for t in range(tiles):
            turn_ref[t, i // SUBLANES, pl.ds(i % SUBLANES, total, stride=SUBLANES), :] = done[
                :, t * LANES : (t + 1) * LANES
            ]
    some = largest_divisor(total, 32)
    for t in range(tiles):
        for e in range(0, total, some):
            halves = [
                turn_ref[t, h, e * SUBLANES : (e + some) * SUBLANES].reshape(some, SUBLANES, LANES)
                for h in range(rows // SUBLANES)
            ]
            out_ref[e : e + some, :, t * LANES : (t + 1) * LANES] = jnp.concatenate(halves, axis=1).astype(BF16)


def params(grid, mib):
    return pltpu.CompilerParams(
        vmem_limit_bytes=mib * MIB, dimension_semantics=("arbitrary",) * len(grid)
    )


def first_step(tokens, factor, twiddle, at, count, sources):
    channels, rows, order = tokens.shape
    width = order // sources
    pack = LANES // width
    per = pack * largest_divisor(count // pack, FIRST // pack)
    grid = (count // per,)
    return pl.pallas_call(
        partial(first_kernel, pack, width),
        grid=grid,
        in_specs=[
            pl.BlockSpec((per, rows, order), lambda n: (at // per + n, 0, 0)),
            pl.BlockSpec(factor.shape, lambda n: (0, 0)),
            pl.BlockSpec(twiddle.shape, lambda n: (0, 0)),
        ],
        out_specs=pl.BlockSpec((sources, per // pack, rows, LANES), lambda n: (0, n, 0, 0)),
        out_shape=jax.ShapeDtypeStruct((sources, count // pack, rows, LANES), BF16),
        compiler_params=params(grid, 60),
        cost_estimate=pl.CostEstimate(
            flops=2 * count * rows * order * order, bytes_accessed=4 * count * rows * order, transcendentals=0
        ),
        name="first_factor",
    )(tokens, factor, twiddle)


def middle_step(received, kernel, second, back, twiddle, offset, at, count, dests):
    sources, _, rows, _ = received.shape
    channels, width, size = kernel.shape
    pack = LANES // width
    per = GROUPS
    groups = count // pack
    grid = (groups // per,)
    out_rows = size // dests
    return pl.pallas_call(
        partial(middle_kernel, pack),
        grid=grid,
        in_specs=[
            pl.BlockSpec((sources, per, rows, LANES), lambda n: (0, offset // (per * pack) + n, 0, 0)),
            pl.BlockSpec((per * pack, width, size), lambda n: (at // (per * pack) + n, 0, 0)),
            pl.BlockSpec(second.shape, lambda n: (0, 0)),
            pl.BlockSpec(back.shape, lambda n: (0, 0)),
            pl.BlockSpec(twiddle.shape, lambda n: (0, 0)),
        ],
        out_specs=pl.BlockSpec((dests, out_rows, per, LANES), lambda n: (0, 0, n, 0)),
        out_shape=jax.ShapeDtypeStruct((dests, out_rows, groups, LANES), BF16),
        scratch_shapes=[pltpu.VMEM((size * per, LANES), F32)],
        compiler_params=params(grid, 32),
        cost_estimate=pl.CostEstimate(
            flops=4 * groups * LANES * size * size, bytes_accessed=6 * groups * LANES * size, transcendentals=0
        ),
        name="outer_factors",
    )(received, kernel, second, back, twiddle)


def turn_step(gating, pack, at, count):
    parts, _, rows, order = gating.shape
    per = GROUPS * pack
    grid = (parts, count // per)
    return pl.pallas_call(
        partial(turn_kernel, pack),
        grid=grid,
        in_specs=[pl.BlockSpec((1, per, rows, order), lambda x, n: (x, at // per + n, 0, 0))],
        out_specs=pl.BlockSpec((1, 1, pack, rows, GROUPS, order), lambda x, n: (x, n, 0, 0, 0, 0)),
        out_shape=jax.ShapeDtypeStruct((parts, count // per, pack, rows, GROUPS, order), BF16),
        scratch_shapes=[pltpu.VMEM((order // LANES, per * rows, LANES), F32)],
        compiler_params=params(grid, 32),
        cost_estimate=pl.CostEstimate(
            flops=parts * count * rows * order, bytes_accessed=4 * parts * count * rows * order, transcendentals=0
        ),
        name="turn_gating",
    )(gating)


def last_step(returned, factor, gating, sources):
    _, parts, rows, groups, _ = returned.shape
    order = factor.shape[0]
    width = order // sources
    pack = LANES // width
    per = GROUPS
    grid = (parts, groups // per)
    block = (1, 1, pack, rows, per, order)
    return pl.pallas_call(
        partial(last_kernel, pack, width),
        grid=grid,
        in_specs=[
            pl.BlockSpec((sources, 1, rows, per, LANES), lambda x, n: (0, x, 0, n, 0)),
            pl.BlockSpec(factor.shape, lambda x, n: (0, 0)),
            pl.BlockSpec(block, lambda x, n: (x, n, 0, 0, 0, 0)),
        ],
        out_specs=pl.BlockSpec(block, lambda x, n: (x, n, 0, 0, 0, 0)),
        out_shape=jax.ShapeDtypeStruct((parts, groups // per, pack, rows, per, order), BF16),
        scratch_shapes=[pltpu.VMEM((pack, rows * per, order), BF16)],
        compiler_params=params(grid, 32),
        cost_estimate=pl.CostEstimate(
            flops=2 * parts * groups * pack * rows * order * order,
            bytes_accessed=6 * parts * groups * pack * rows * order,
            transcendentals=0,
        ),
        name="last_factor",
    )(returned, factor, gating)


def project_step(gated, projection):
    _, _, _, rows, _, order = gated[0].shape
    total = projection.shape[0]
    step = 2 * LANES
    grid = (order // step,)
    return pl.pallas_call(
        partial(project_kernel, len(gated)),
        grid=grid,
        in_specs=[
            pl.BlockSpec(part.shape[:-1] + (step,), lambda n: (0, 0, 0, 0, 0, n)) for part in gated
        ]
        + [pl.BlockSpec(projection.shape, lambda n: (0, 0))],
        out_specs=pl.BlockSpec((total, rows, step), lambda n: (0, 0, n)),
        out_shape=jax.ShapeDtypeStruct((total, rows, order), BF16),
        scratch_shapes=[
            pltpu.VMEM((step // LANES, rows // SUBLANES, total * SUBLANES, LANES), F32),
        ],
        compiler_params=params(grid, 28),
        cost_estimate=pl.CostEstimate(
            flops=2 * total * total * rows * order, bytes_accessed=4 * total * rows * order, transcendentals=0
        ),
        name="projection",
    )(*gated, projection)


def spans(sizes):
    at = 0
    for size in sizes:
        yield at, size
        at += size


def chunked(
    tokens,
    gating,
    kernel,
    first_factor,
    first_twiddle,
    second_factor,
    inverse_second,
    inverse_twiddle,
    inverse_first,
    projection,
):
    sources, parts = lax.axis_size("seq"), lax.axis_size("chan")
    dests = sources * parts
    channels, _, order = tokens.shape
    width = order // sources
    pack = LANES // width
    unit = GROUPS * pack
    units = channels // unit
    total, out_rows, _ = gating.shape
    inverse_first = inverse_first.T
    twiddle_back = jnp.tile(inverse_twiddle.T, (1, pack))
    projection = projection.T.reshape(total, total // unit, GROUPS, pack)
    projection = projection.transpose(0, 1, 3, 2).reshape(total, total)
    there = [unit, channels - unit] if units > 1 else [unit]
    back = [unit, channels - 2 * unit, unit] if units > 2 else [unit] * units

    gating = gating.reshape(parts, channels, out_rows, order)
    turned = [turn_step(gating, pack, at, count) for at, count in spans(back)]
    starts, arrived = [], []

    def exchange(sent, axes):
        if arrived:
            sent, arrived[-1] = lax.optimization_barrier((sent, arrived[-1]))
        arrived.append(lax.all_to_all(sent, axes, split_axis=0, concat_axis=0, tiled=True))

    for at, count in spans(there):
        starts.append(at)
        exchange(first_step(tokens, first_factor, first_twiddle, at, count, sources), "seq")
    for at, count in spans(back):
        n = max(n for n, start in enumerate(starts) if start <= at)
        sent = middle_step(
            arrived[n], kernel, second_factor, inverse_second, twiddle_back, at - starts[n], at, count, dests
        )
        if at > 0 and at + count == channels:
            sent, turned = lax.optimization_barrier((sent, turned))
        exchange(sent, ("seq", "chan"))
    returned = arrived[len(there) :]
    gated = []
    for count, block, gate in zip(back, returned, turned, strict=True):
        block = block.reshape(sources, parts, out_rows, count // pack, LANES)
        gated.append(last_step(block, inverse_first, gate, sources))
    return project_step(gated, projection)


def plain(
    tokens,
    gating,
    kernel,
    first_factor,
    first_twiddle,
    second_factor,
    inverse_second,
    inverse_twiddle,
    inverse_first,
    projection,
):
    seq_count = lax.axis_size("seq")
    chan_count = lax.axis_size("chan")
    channels, local_rows, order_inner = tokens.shape
    order_outer = second_factor.shape[0]
    block_cols = order_inner // seq_count
    chan_rows = local_rows // chan_count
    first_split = first_factor.reshape(seq_count, block_cols, order_inner)
    forward = jnp.einsum("cab,skb->scka", tokens, first_split, preferred_element_type=jnp.float32)
    twiddle = first_twiddle.reshape(local_rows, seq_count, block_cols).transpose(1, 2, 0)
    forward = (forward * twiddle[:, None]).astype(jnp.bfloat16)
    forward = forward.reshape(seq_count, 1, channels, block_cols * local_rows)
    received = lax.all_to_all(forward, "seq", split_axis=0, concat_axis=1, tiled=True)
    received = received.reshape(seq_count, channels, block_cols, local_rows)
    second_split = second_factor.reshape(order_outer, seq_count, local_rows)
    spectrum = jnp.einsum(
        "scka,jsa->ckj", received, second_split, preferred_element_type=jnp.float32
    )
    scaled = (spectrum * kernel).astype(jnp.bfloat16)
    first_join = inverse_first.reshape(order_inner, seq_count, block_cols)
    inverse_split = inverse_second.reshape(seq_count, local_rows, order_outer)
    inverse = jnp.einsum("ckj,sij->scki", scaled, inverse_split, preferred_element_type=jnp.float32)
    twiddle_back = inverse_twiddle.reshape(block_cols, seq_count, local_rows).transpose(1, 0, 2)
    inverse = (inverse * twiddle_back[:, None]).astype(jnp.bfloat16)
    inverse = inverse.reshape(seq_count, 1, channels, block_cols * local_rows)
    returned = lax.all_to_all(inverse, "seq", split_axis=0, concat_axis=1, tiled=True)
    returned = returned.reshape(seq_count, channels, block_cols, local_rows)
    mixed_rows = jnp.einsum(
        "scki,bsk->cib", returned, first_join, preferred_element_type=jnp.float32
    ).astype(jnp.bfloat16)
    mixed_rows = mixed_rows.reshape(channels, chan_count, chan_rows, order_inner)
    mixed_rows = lax.all_to_all(mixed_rows, "chan", split_axis=1, concat_axis=0, tiled=True)
    mixed_rows = mixed_rows.reshape(channels * chan_count, chan_rows, order_inner)
    gated_rows = (mixed_rows.astype(jnp.float32) * gating.astype(jnp.float32)).astype(jnp.bfloat16)
    result_rows = jnp.einsum(
        "cab,ce->eab", gated_rows, projection, preferred_element_type=jnp.float32
    )
    return result_rows.astype(jnp.bfloat16)


def body(*arrays):
    tokens, gating = arrays[:2]
    width = tokens.shape[2] // lax.axis_size("seq")
    whole_tiles = gating.shape[1] % 16 == 0 and tokens.shape[1] % 16 == 0 and LANES % width == 0
    whole_tiles = whole_tiles and tokens.shape[0] % (GROUPS * LANES // width) == 0
    return chunked(*arrays) if whole_tiles else plain(*arrays)


def solution(mesh):
    return jax.shard_map(
        body,
        mesh=mesh,
        in_specs=(
            P("chan", "seq", None),
            P(None, ("seq", "chan"), None),
            P("chan", "seq", None),
            P(),
            P("seq", None),
            P(),
            P(),
            P("seq", None),
            P(),
            P(),
        ),
        out_specs=P(None, ("seq", "chan"), None),
        check_vma=False,
    )
```

```python
from functools import partial

import jax
import jax.numpy as jnp
from jax import lax
from jax.experimental import pallas as pl
from jax.experimental.pallas import tpu as pltpu
from jax.sharding import PartitionSpec as P

LANES = 128
SUBLANES = 8
GROUPS = 16
FIRST = 16
MIB = 1024 * 1024
F32 = jnp.float32
BF16 = jnp.bfloat16


def largest_divisor(number, most):
    return max(d for d in range(1, min(number, most) + 1) if number % d == 0)


def dot_nt(left, right):
    return lax.dot_general(left, right, (((1,), (1,)), ((), ())), preferred_element_type=F32)


def regroup(tiles, width):
    count = len(tiles)
    if count == 1:
        return list(tiles)
    lane = lax.broadcasted_iota(jnp.int32, tiles[0].shape, tiles[0].ndim - 1)
    out = []
    for q in range(count):
        tile = None
        for r in range(count):
            shift = ((r - q) * width) % LANES
            moved = pltpu.roll(tiles[r], shift, tiles[r].ndim - 1) if shift else tiles[r]
            tile = moved if tile is None else jnp.where(lane >= r * width, moved, tile)
        out.append(tile)
    return out


def first_kernel(pack, width, tokens_ref, factor_ref, twiddle_ref, out_ref):
    channels, rows, order = tokens_ref.shape
    groups = channels // pack
    left = tokens_ref[...].reshape(channels * rows, order)
    step = 2 * LANES
    for at in range(0, order, step):
        part = dot_nt(left, factor_ref[at : at + step, :])
        part = part.reshape(channels, rows, step) * twiddle_ref[:, at : at + step][None]
        for half in range(step // LANES):
            tile = part[:, :, half * LANES : (half + 1) * LANES].reshape(groups, pack, rows, LANES)
            moved = regroup([tile[:, r].reshape(groups * rows, LANES) for r in range(pack)], width)
            base = (at // LANES + half) * pack
            for q in range(pack):
                out_ref[base + q] = moved[q].astype(BF16).reshape(groups, rows, LANES)


def middle_kernel(pack, recv_ref, kernel_ref, second_ref, back_ref, twiddle_ref, out_ref, turn_ref):
    size = second_ref.shape[0]
    groups = recv_ref.shape[1]
    width = kernel_ref.shape[1]
    both = 2 if groups % 2 == 0 else 1
    for at in range(0, groups, both):
        cols = [recv_ref[:, at + p].reshape(size, LANES) for p in range(both)]
        spectrum = jnp.dot(
            second_ref[...], jnp.concatenate(cols, axis=1), preferred_element_type=F32
        )
        kern = [
            kernel_ref[(at + p) * pack : (at + p + 1) * pack].reshape(pack * width, size).astype(F32).T
            for p in range(both)
        ]
        scaled = (spectrum * jnp.concatenate(kern, axis=1)).astype(BF16)
        inverse = jnp.dot(back_ref[...], scaled, preferred_element_type=F32)
        for p in range(both):
            part = inverse[:, p * LANES : (p + 1) * LANES] * twiddle_ref[...]
            turn_ref[pl.ds(at + p, size, stride=groups), :] = part
    out_ref[...] = turn_ref[...].astype(BF16).reshape(out_ref.shape)


def turn_kernel(pack, gating_ref, out_ref, turn_ref):
    _, channels, rows, order = gating_ref.shape
    groups = channels // pack
    for t in range(order // LANES):
        lanes = slice(t * LANES, (t + 1) * LANES)
        turn_ref[t] = gating_ref[0, :, :, lanes].astype(F32).reshape(channels * rows, LANES)
        for r in range(pack):
            for i in range(rows):
                part = turn_ref[t, pl.ds(r * rows + i, groups, stride=pack * rows), :]
                out_ref[0, 0, r, i, :, lanes] = part.astype(BF16)


def last_kernel(pack, width, recv_ref, factor_ref, gating_ref, out_ref, wide_ref):
    sources, _, rows, groups, _ = recv_ref.shape
    order = factor_ref.shape[0]
    widen(pack, width, recv_ref.at[:, 0], wide_ref)
    left = wide_ref[...].reshape(pack * rows * groups, order)
    step = 2 * LANES
    for at in range(0, order, step):
        mixed = jnp.dot(left, factor_ref[:, at : at + step], preferred_element_type=F32)
        mixed = mixed.astype(BF16).astype(F32)
        mixed = mixed.reshape(pack, rows, groups, step)
        gated = mixed * gating_ref[0, 0, :, :, :, at : at + step].astype(F32)
        out_ref[0, 0, :, :, :, at : at + step] = gated.astype(BF16)


def widen(pack, width, recv, wide_ref):
    sources, rows, groups, _ = recv.shape
    for t in range(sources // pack):
        tiles = [recv[t * pack + r].astype(F32).reshape(rows * groups, LANES) for r in range(pack)]
        moved = regroup(tiles, width)
        for q in range(pack):
            wide_ref[q, :, t * LANES : (t + 1) * LANES] = moved[q].astype(BF16)


def project_kernel(count, *refs):
    gated_refs, (projection_ref, out_ref, turn_ref) = refs[:count], refs[count:]
    parts, _, pack, rows, _, step = gated_refs[0].shape
    total = projection_ref.shape[0]
    tiles = step // LANES
    for i in range(rows):
        right = jnp.concatenate(
            [
                ref[x, n, r, i]
                for x in range(parts)
                for ref in gated_refs
                for n in range(ref.shape[1])
                for r in range(pack)
            ],
            axis=0,
        )
        done = jnp.dot(projection_ref[...], right, preferred_element_type=F32)
        for t in range(tiles):
            turn_ref[t, i // SUBLANES, pl.ds(i % SUBLANES, total, stride=SUBLANES), :] = done[
                :, t * LANES : (t + 1) * LANES
            ]
    some = largest_divisor(total, 32)
    for t in range(tiles):
        for e in range(0, total, some):
            halves = [
                turn_ref[t, h, e * SUBLANES : (e + some) * SUBLANES].reshape(some, SUBLANES, LANES)
                for h in range(rows // SUBLANES)
            ]
            out_ref[e : e + some, :, t * LANES : (t + 1) * LANES] = jnp.concatenate(halves, axis=1).astype(BF16)


def params(grid, mib):
    return pltpu.CompilerParams(
        vmem_limit_bytes=mib * MIB, dimension_semantics=("arbitrary",) * len(grid)
    )


def first_step(tokens, factor, twiddle, at, count, sources):
    channels, rows, order = tokens.shape
    width = order // sources
    pack = LANES // width
    per = pack * largest_divisor(count // pack, FIRST // pack)
    grid = (count // per,)
    return pl.pallas_call(
        partial(first_kernel, pack, width),
        grid=grid,
        in_specs=[
            pl.BlockSpec((per, rows, order), lambda n: (at // per + n, 0, 0)),
            pl.BlockSpec(factor.shape, lambda n: (0, 0)),
            pl.BlockSpec(twiddle.shape, lambda n: (0, 0)),
        ],
        out_specs=pl.BlockSpec((sources, per // pack, rows, LANES), lambda n: (0, n, 0, 0)),
        out_shape=jax.ShapeDtypeStruct((sources, count // pack, rows, LANES), BF16),
        compiler_params=params(grid, 60),
        cost_estimate=pl.CostEstimate(
            flops=2 * count * rows * order * order, bytes_accessed=4 * count * rows * order, transcendentals=0
        ),
        name="first_factor",
    )(tokens, factor, twiddle)


def middle_step(received, kernel, second, back, twiddle, offset, at, count, dests):
    sources, _, rows, _ = received.shape
    channels, width, size = kernel.shape
    pack = LANES // width
    per = GROUPS
    groups = count // pack
    grid = (groups // per,)
    out_rows = size // dests
    return pl.pallas_call(
        partial(middle_kernel, pack),
        grid=grid,
        in_specs=[
            pl.BlockSpec((sources, per, rows, LANES), lambda n: (0, offset // (per * pack) + n, 0, 0)),
            pl.BlockSpec((per * pack, width, size), lambda n: (at // (per * pack) + n, 0, 0)),
            pl.BlockSpec(second.shape, lambda n: (0, 0)),
            pl.BlockSpec(back.shape, lambda n: (0, 0)),
            pl.BlockSpec(twiddle.shape, lambda n: (0, 0)),
        ],
        out_specs=pl.BlockSpec((dests, out_rows, per, LANES), lambda n: (0, 0, n, 0)),
        out_shape=jax.ShapeDtypeStruct((dests, out_rows, groups, LANES), BF16),
        scratch_shapes=[pltpu.VMEM((size * per, LANES), F32)],
        compiler_params=params(grid, 32),
        cost_estimate=pl.CostEstimate(
            flops=4 * groups * LANES * size * size, bytes_accessed=6 * groups * LANES * size, transcendentals=0
        ),
        name="outer_factors",
    )(received, kernel, second, back, twiddle)


def turn_step(gating, pack, at, count):
    parts, _, rows, order = gating.shape
    per = GROUPS * pack
    grid = (parts, count // per)
    return pl.pallas_call(
        partial(turn_kernel, pack),
        grid=grid,
        in_specs=[pl.BlockSpec((1, per, rows, order), lambda x, n: (x, at // per + n, 0, 0))],
        out_specs=pl.BlockSpec((1, 1, pack, rows, GROUPS, order), lambda x, n: (x, n, 0, 0, 0, 0)),
        out_shape=jax.ShapeDtypeStruct((parts, count // per, pack, rows, GROUPS, order), BF16),
        scratch_shapes=[pltpu.VMEM((order // LANES, per * rows, LANES), F32)],
        compiler_params=params(grid, 32),
        cost_estimate=pl.CostEstimate(
            flops=parts * count * rows * order, bytes_accessed=4 * parts * count * rows * order, transcendentals=0
        ),
        name="turn_gating",
    )(gating)


def last_step(returned, factor, gating, sources):
    _, parts, rows, groups, _ = returned.shape
    order = factor.shape[0]
    width = order // sources
    pack = LANES // width
    per = GROUPS
    grid = (parts, groups // per)
    block = (1, 1, pack, rows, per, order)
    return pl.pallas_call(
        partial(last_kernel, pack, width),
        grid=grid,
        in_specs=[
            pl.BlockSpec((sources, 1, rows, per, LANES), lambda x, n: (0, x, 0, n, 0)),
            pl.BlockSpec(factor.shape, lambda x, n: (0, 0)),
            pl.BlockSpec(block, lambda x, n: (x, n, 0, 0, 0, 0)),
        ],
        out_specs=pl.BlockSpec(block, lambda x, n: (x, n, 0, 0, 0, 0)),
        out_shape=jax.ShapeDtypeStruct((parts, groups // per, pack, rows, per, order), BF16),
        scratch_shapes=[pltpu.VMEM((pack, rows * per, order), BF16)],
        compiler_params=params(grid, 32),
        cost_estimate=pl.CostEstimate(
            flops=2 * parts * groups * pack * rows * order * order,
            bytes_accessed=6 * parts * groups * pack * rows * order,
            transcendentals=0,
        ),
        name="last_factor",
    )(returned, factor, gating)


def project_step(gated, projection):
    _, _, _, rows, _, order = gated[0].shape
    total = projection.shape[0]
    step = 2 * LANES
    grid = (order // step,)
    return pl.pallas_call(
        partial(project_kernel, len(gated)),
        grid=grid,
        in_specs=[
            pl.BlockSpec(part.shape[:-1] + (step,), lambda n: (0, 0, 0, 0, 0, n)) for part in gated
        ]
        + [pl.BlockSpec(projection.shape, lambda n: (0, 0))],
        out_specs=pl.BlockSpec((total, rows, step), lambda n: (0, 0, n)),
        out_shape=jax.ShapeDtypeStruct((total, rows, order), BF16),
        scratch_shapes=[
            pltpu.VMEM((step // LANES, rows // SUBLANES, total * SUBLANES, LANES), F32),
        ],
        compiler_params=params(grid, 28),
        cost_estimate=pl.CostEstimate(
            flops=2 * total * total * rows * order, bytes_accessed=4 * total * rows * order, transcendentals=0
        ),
        name="projection",
    )(*gated, projection)


def spans(sizes):
    at = 0
    for size in sizes:
        yield at, size
        at += size


def chunked(
    tokens,
    gating,
    kernel,
    first_factor,
    first_twiddle,
    second_factor,
    inverse_second,
    inverse_twiddle,
    inverse_first,
    projection,
):
    sources, parts = lax.axis_size("seq"), lax.axis_size("chan")
    dests = sources * parts
    channels, _, order = tokens.shape
    width = order // sources
    pack = LANES // width
    unit = GROUPS * pack
    units = channels // unit
    total, out_rows, _ = gating.shape
    inverse_first = inverse_first.T
    twiddle_back = jnp.tile(inverse_twiddle.T, (1, pack))
    projection = projection.T.reshape(total, total // unit, GROUPS, pack)
    projection = projection.transpose(0, 1, 3, 2).reshape(total, total)
    there = [unit, channels - unit] if units > 1 else [unit]
    back = [unit, channels - 2 * unit, unit] if units > 2 else [unit] * units

    gating = gating.reshape(parts, channels, out_rows, order)
    turned = [turn_step(gating, pack, at, count) for at, count in spans(back)]
    starts, arrived = [], []

    def exchange(sent, axes):
        if arrived and len(arrived) != len(there) + 1:
            sent, arrived[-1] = lax.optimization_barrier((sent, arrived[-1]))
        arrived.append(lax.all_to_all(sent, axes, split_axis=0, concat_axis=0, tiled=True))

    for at, count in spans(there):
        starts.append(at)
        exchange(first_step(tokens, first_factor, first_twiddle, at, count, sources), "seq")
    for at, count in spans(back):
        n = max(n for n, start in enumerate(starts) if start <= at)
        sent = middle_step(
            arrived[n], kernel, second_factor, inverse_second, twiddle_back, at - starts[n], at, count, dests
        )
        if at > 0 and at + count == channels:
            sent, turned = lax.optimization_barrier((sent, turned))
        exchange(sent, ("seq", "chan"))
    returned = arrived[len(there) :]
    gated = []
    for count, block, gate in zip(back, returned, turned, strict=True):
        block = block.reshape(sources, parts, out_rows, count // pack, LANES)
        gated.append(last_step(block, inverse_first, gate, sources))
    return project_step(gated, projection)


def plain(
    tokens,
    gating,
    kernel,
    first_factor,
    first_twiddle,
    second_factor,
    inverse_second,
    inverse_twiddle,
    inverse_first,
    projection,
):
    seq_count = lax.axis_size("seq")
    chan_count = lax.axis_size("chan")
    channels, local_rows, order_inner = tokens.shape
    order_outer = second_factor.shape[0]
    block_cols = order_inner // seq_count
    chan_rows = local_rows // chan_count
    first_split = first_factor.reshape(seq_count, block_cols, order_inner)
    forward = jnp.einsum("cab,skb->scka", tokens, first_split, preferred_element_type=jnp.float32)
    twiddle = first_twiddle.reshape(local_rows, seq_count, block_cols).transpose(1, 2, 0)
    forward = (forward * twiddle[:, None]).astype(jnp.bfloat16)
    forward = forward.reshape(seq_count, 1, channels, block_cols * local_rows)
    received = lax.all_to_all(forward, "seq", split_axis=0, concat_axis=1, tiled=True)
    received = received.reshape(seq_count, channels, block_cols, local_rows)
    second_split = second_factor.reshape(order_outer, seq_count, local_rows)
    spectrum = jnp.einsum(
        "scka,jsa->ckj", received, second_split, preferred_element_type=jnp.float32
    )
    scaled = (spectrum * kernel).astype(jnp.bfloat16)
    first_join = inverse_first.reshape(order_inner, seq_count, block_cols)
    inverse_split = inverse_second.reshape(seq_count, local_rows, order_outer)
    inverse = jnp.einsum("ckj,sij->scki", scaled, inverse_split, preferred_element_type=jnp.float32)
    twiddle_back = inverse_twiddle.reshape(block_cols, seq_count, local_rows).transpose(1, 0, 2)
    inverse = (inverse * twiddle_back[:, None]).astype(jnp.bfloat16)
    inverse = inverse.reshape(seq_count, 1, channels, block_cols * local_rows)
    returned = lax.all_to_all(inverse, "seq", split_axis=0, concat_axis=1, tiled=True)
    returned = returned.reshape(seq_count, channels, block_cols, local_rows)
    mixed_rows = jnp.einsum(
        "scki,bsk->cib", returned, first_join, preferred_element_type=jnp.float32
    ).astype(jnp.bfloat16)
    mixed_rows = mixed_rows.reshape(channels, chan_count, chan_rows, order_inner)
    mixed_rows = lax.all_to_all(mixed_rows, "chan", split_axis=1, concat_axis=0, tiled=True)
    mixed_rows = mixed_rows.reshape(channels * chan_count, chan_rows, order_inner)
    gated_rows = (mixed_rows.astype(jnp.float32) * gating.astype(jnp.float32)).astype(jnp.bfloat16)
    result_rows = jnp.einsum(
        "cab,ce->eab", gated_rows, projection, preferred_element_type=jnp.float32
    )
    return result_rows.astype(jnp.bfloat16)


def body(*arrays):
    tokens, gating = arrays[:2]
    width = tokens.shape[2] // lax.axis_size("seq")
    whole_tiles = gating.shape[1] % 16 == 0 and tokens.shape[1] % 16 == 0 and LANES % width == 0
    whole_tiles = whole_tiles and tokens.shape[0] % (GROUPS * LANES // width) == 0
    return chunked(*arrays) if whole_tiles else plain(*arrays)


def solution(mesh):
    return jax.shard_map(
        body,
        mesh=mesh,
        in_specs=(
            P("chan", "seq", None),
            P(None, ("seq", "chan"), None),
            P("chan", "seq", None),
            P(),
            P("seq", None),
            P(),
            P(),
            P("seq", None),
            P(),
            P(),
        ),
        out_specs=P(None, ("seq", "chan"), None),
        check_vma=False,
    )
```
